32 devices in a mesh: groups: 2 (over y), block: 4 (over z), term: 2 (over x), half: 2 (over core).
Axes of the slice: x: 2, y: 2, z: 4, core: 2. Of those that a mesh axis runs over, the one named last changes fastest.
Arguments:
- psi_blocks: bfloat16 [256, 256, 256], P(('groups', 'block'), 'half'), parts along dimension 0, may hold values from -6 to 6
- left_env: bfloat16 [16, 4, 256, 256], P(('groups', 'term'), 'block', 'half'), parts along dimension 0, may hold values from -0.375 to 0.375
- right_env: bfloat16 [16, 4, 256, 256], P(('groups', 'term'), 'block'), parts along dimension 0, may hold values from -0.375 to 0.375
- right_owner: int32 [256, 1], P('groups'), parts along dimension 0, may hold values from 0 to 3; in each aligned block of 32 rows (0 to 31, 32 to 63, ...) at most 16 rows name the same one
Outputs:
- hpsi: bfloat16 [512, 256, 256], P(('groups', 'block', 'term'), 'half'), parts along dimension 0
The draws below stay inside these ranges and needn't reach their ends.
There are 2 independent parts, one for each index of `groups`. The reference program is written for one: setup_inputs(seed, part) draws one part's arguments, and reference() takes and returns one part's arrays. A program takes and returns all parts, laid end to end along the dimension named above; each array names one. Nothing has to cross between parts.
Inputs may be any that keep to these rules, and one draw needn't show every extreme that they name: `right_owner`: among the 32 blocks of one left sector at most 16 have the same right sector, and in every draw some left sector has exactly 16 blocks with one right sector; every right sector occurs.
All inputs are finite; a program needn't handle non-finite values.
Results may differ from the reference program's by a relative error of at most 0.0059.
Values may be sent and summed in bfloat16 or wider, within the bound.
A program may use at most 128 MiB of HBM per device.

```python
import math
import jax
import jax.numpy as jnp
import numpy as np
from jax import lax

BLK = 256
BLOCKS_DEV = 32
TERMS = 8
SECTORS = 4
CAP = 16
SLOTS = 128
N_TERM = 2


def block_scale(own_key, dims, pieces, least, top_value):
    level = 1.0
    for axis_at, shards_of in pieces:
        steps = jax.random.uniform(jax.random.fold_in(jax.random.fold_in(own_key, 6), axis_at), (shards_of,), jnp.float32, least / len(pieces), top_value / len(pieces))
        level = level * jnp.repeat(jnp.exp(steps), dims[axis_at] // shards_of).reshape((-1,) + (1,) * (len(dims) - 1 - axis_at))
    return level


def routed_block(stream_key, own, number, rows, count, top, most, skew):
    order = jax.random.permutation(stream_key, count)
    crowded, common = shares(count, rows * top, most, skew, True), shares(count, rows * top, most, skew, False)
    places = jnp.arange(count)

    def named(sizes, offset_by):
        used = int((sizes > 0).sum())
        fixed = max(1, used // 4)
        passed = fixed + (places - fixed + offset_by * (used - fixed)) % max(1, count - fixed)
        return jnp.zeros((count,), jnp.int32).at[order[jnp.where(places < fixed, places, passed)]].set(jnp.asarray(sizes, jnp.int32))

    sizes = jnp.where(number % 4 == 0, named(crowded, number // 4), named(common, number - number // 4 - 1))
    mixed = jax.random.permutation(jax.random.fold_in(own, 3), count)
    giver, receiver = mixed[0:count // 2 * 2:2], mixed[1:count // 2 * 2:2]
    room = jnp.minimum(sizes[giver] - 1, most - sizes[receiver]) // 2
    room = jnp.where((giver == order[0]) | (receiver == order[0]) | (sizes[receiver] == 0), 0, jnp.maximum(room, 0))
    passed = jax.random.randint(jax.random.fold_in(own, 4), (count // 2,), 0, 1 << 20) % (room + 1)
    sizes = sizes.at[giver].add(-passed).at[receiver].add(passed)
    members = jnp.searchsorted(jnp.cumsum(sizes), jnp.arange(rows * top), side="right").astype(jnp.int32)
    grid = members.reshape(top, rows).T
    grid = grid[jax.random.permutation(jax.random.fold_in(own, 1), rows)]
    offset_by = jax.random.randint(jax.random.fold_in(own, 2), (rows, 1), 0, top)
    return jnp.take_along_axis(grid, (jnp.arange(top)[None, :] + offset_by) % top, axis=1)


def shares(amount, total, reach, skew, full):
    weights = [(1 << 20) // math.isqrt(grade ** skew) + 1 for grade in range(1, amount + 1)]
    largest = reach if full else min(reach, max(-(-total // amount), total * weights[0] // sum(weights)))
    least = 1 if total - largest >= amount - 1 else 0
    holding, surplus = [largest] + [least] * (amount - 1), total - largest - least * (amount - 1)
    while surplus > 0:
        movable = [i for i in range(1, amount) if holding[i] < largest] or [i for i in range(1, amount) if holding[i] < reach]
        mass, left = sum([weights[i] for i in movable]), surplus
        for i in movable:
            extra = min(reach - holding[i], max(1, left * weights[i] // mass), surplus)
            holding[i] = holding[i] + extra
            surplus = surplus - extra
    return np.array(holding)


def noise(stream_key, shape, scale, bound, cuts=(), kind=jnp.bfloat16):
    loudness = block_scale(stream_key, shape, cuts, -0.22, 0.18) if cuts else 1.0
    entries = jax.random.normal(stream_key, shape, jnp.float32) * scale * loudness
    return jnp.minimum(jnp.maximum(entries, -bound), bound).astype(kind)


def setup_inputs(seed: int = 0, part: int = 0) -> dict:
    keys = jax.random.split(jax.random.key(seed), 5)
    part_keys = jax.random.split(jax.random.fold_in(keys[4], part), 5)
    psi_blocks = noise(part_keys[0], (SLOTS, BLK, BLK), 1.0, 6.0, ((0, 4), (1, 2)))
    left_env = noise(part_keys[1], (TERMS, SECTORS, BLK, BLK), BLK ** -0.5, 0.375, ((0, 2), (1, 4), (2, 2)))
    right_env = noise(part_keys[2], (TERMS, SECTORS, BLK, BLK), BLK ** -0.5, 0.375, ((0, 2), (1, 4)))
    right_owner_keys = jax.random.split(jax.random.fold_in(part_keys[3], 1), SLOTS // BLOCKS_DEV)
    right_owner_turns = jax.random.permutation(jax.random.fold_in(part_keys[3], 3), SLOTS // BLOCKS_DEV)
    right_owner = jax.vmap(lambda own, number: routed_block(jax.random.fold_in(part_keys[3], 2), own, number, BLOCKS_DEV, SECTORS, 1, CAP, 2))(right_owner_keys, right_owner_turns).reshape((SLOTS, 1))
    return dict(psi_blocks=psi_blocks, left_env=left_env, right_env=right_env, right_owner=right_owner)


def reference(psi_blocks, left_env, right_env, right_owner):
    per_sector = BLOCKS_DEV
    slot_count = psi_blocks.shape[0]
    owners = right_owner[:, 0]
    source = jnp.arange(slot_count, dtype=jnp.int32) // per_sector
    grouped = owners.reshape(-1, per_sector)
    matches = (grouped[:, :, None] == grouped[:, None, :]).astype(jnp.int32)
    position = jnp.arange(per_sector, dtype=jnp.int32)
    earlier_mask = (position[None, :] < position[:, None]).astype(jnp.int32)
    ranking = jnp.sum(matches * earlier_mask[None], axis=2).reshape(-1).astype(jnp.int32)
    target = ((owners * SECTORS + source) * CAP + ranking).astype(jnp.int32)
    psi_wide = psi_blocks.astype(jnp.float32)
    per_group = TERMS // N_TERM
    summed = jnp.zeros((slot_count, BLK, BLK), jnp.float32)
    for term_group in range(N_TERM):
        partial_value = jnp.zeros((slot_count, BLK, BLK), jnp.float32)
        for inner_term in range(per_group):
            term_index = term_group * per_group + inner_term
            left_block = left_env[term_index].astype(jnp.float32)[source]
            blended = jnp.einsum("sik,skc->sic", left_block, psi_wide)
            blended = lax.optimization_barrier(blended.astype(jnp.bfloat16)).astype(jnp.float32)
            right_block = right_env[term_index].astype(jnp.float32)[owners]
            partial_value = partial_value + jnp.einsum("sic,scn->sin", blended, right_block)
        partial_value = lax.optimization_barrier(partial_value.astype(jnp.bfloat16)).astype(jnp.float32)
        summed = summed + partial_value
    result = jnp.zeros((SECTORS * SECTORS * CAP, BLK, BLK), jnp.bfloat16)
    return result.at[target].set(summed.astype(jnp.bfloat16))
```

```python
import functools

import jax
import jax.numpy as jnp
from jax import lax
from jax.experimental import pallas as pl
from jax.experimental.pallas import tpu as pltpu
from jax.sharding import PartitionSpec as P

MESH = pl.DeviceIdType.MESH
STEP = 1
AHEAD = 3


def slot_sources(right_owner, per_sector, n_block, capacity):
    source = lax.axis_index("block")
    targets = lax.dynamic_slice_in_dim(right_owner[:, 0], source * per_sector, per_sector)
    position = jnp.arange(per_sector, dtype=jnp.int32)
    upto = position[:, None] >= position[None, :]
    named = targets[None, :] == jnp.arange(n_block, dtype=jnp.int32)[:, None]
    count = jnp.sum((named[:, None, :] & upto[None]).astype(jnp.int32), axis=2)
    order = jnp.arange(capacity, dtype=jnp.int32)
    return jnp.sum((count[:, None, :] <= order[None, :, None]).astype(jnp.int32), axis=2).reshape(-1)


def kernel(
    n_block, capacity,
    idx, psi, left, right, out,
    stage, buf, lall, rall, mixed,
    z_send, z_recv, x_send, x_recv, s_send, s_recv,
    lz_send, lz_recv, lx_send, lx_recv, r_send, r_recv,
):
    z, x, h = lax.axis_index("block"), lax.axis_index("term"), lax.axis_index("half")
    per_sector, rows, width = psi.shape
    here = left.shape[0]
    terms = 2 * here
    share = capacity // 2
    steps = share // STEP
    per_core = here // 2
    owned = n_block // 2

    def remote(src, dst, send, recv, **where):
        return pltpu.make_async_remote_copy(
            src_ref=src, dst_ref=dst, send_sem=send, recv_sem=recv,
            device_id=where, device_id_type=MESH,
        )

    barrier = pltpu.get_barrier_semaphore()
    for d in range(1, n_block):
        pl.semaphore_signal(
            barrier, inc=1, device_id={"block": lax.rem(z + d, n_block)}, device_id_type=MESH)
    pl.semaphore_signal(barrier, inc=1, device_id={"term": 1 - x}, device_id_type=MESH)
    pl.semaphore_signal(barrier, inc=1, device_id={"half": 1 - h}, device_id_type=MESH)

    my_rows = pl.ds(pl.multiple_of(h * rows, rows), rows)
    other_rows = pl.ds(pl.multiple_of((1 - h) * rows, rows), rows)

    def slot(a, column, i, which):
        return buf.at[a, pl.ds(column * share + i * STEP, STEP), which, :]

    def l_part(a, column):
        return lall.at[a, pl.ds(column * here, here)]

    def l_up(a, src):
        return remote(src, l_part(a, x), lz_send.at[0, a], lz_recv.at[a], block=z + 1)

    def l_down(a, src):
        return remote(src, l_part(a, x), lz_send.at[1, a], lz_recv.at[a], block=z - 1)

    def l_cross(a, src):
        return remote(src, l_part(a, x), lx_send.at[lax.rem(a, owned)], lx_recv.at[lax.rem(a, owned)], term=1 - x)

    def l_cross_in(q):
        return remote(
            l_part(x * owned + q, 1 - x), l_part(x * owned + q, 1 - x), lx_send.at[q], lx_recv.at[q], term=1 - x)

    def pass_left(d):
        @pl.when(z - d >= 0)
        def _():
            a = z - d
            l_up(a, l_part(a, x)).wait_recv()

            @pl.when(z < n_block - 1)
            def _():
                l_up(a, l_part(a, x)).start()

            @pl.when(a // owned != x)
            def _():
                l_cross(a, l_part(a, x)).start()

        @pl.when(z + d < n_block)
        def _():
            a = z + d
            l_down(a, l_part(a, x)).wait_recv()

            @pl.when(z > 0)
            def _():
                l_down(a, l_part(a, x)).start()

            @pl.when(a // owned != x)
            def _():
                l_cross(a, l_part(a, x)).start()

    def r_part(column, core):
        return rall.at[pl.ds(column * here + core * per_core, per_core)]

    def r_cross():
        return remote(
            right.at[pl.ds(h * per_core, per_core)], r_part(x, h), r_send.at[0], r_recv.at[0], term=1 - x)

    def r_cross_in():
        return remote(r_part(1 - x, h), r_part(1 - x, h), r_send.at[0], r_recv.at[0], term=1 - x)

    def r_sibling():
        return remote(r_part(1 - x, h), r_part(1 - x, h), r_send.at[1], r_recv.at[1], half=1 - h)

    def r_sibling_in():
        return remote(r_part(1 - x, 1 - h), r_part(1 - x, 1 - h), r_send.at[1], r_recv.at[1], half=1 - h)

    def psi_out(d, i):
        b = lax.rem(z + d, n_block)
        return remote(
            stage.at[d - 1, pl.ds(i * STEP, STEP)], slot(z, x, i, my_rows),
            z_send.at[d - 1, i], z_recv.at[d - 1, i], block=b)

    def psi_in(d, i):
        a = lax.rem(z + n_block - d, n_block)
        return remote(
            stage.at[d - 1, pl.ds(i * STEP, STEP)], slot(a, x, i, my_rows),
            z_send.at[d - 1, i], z_recv.at[d - 1, i], block=a)

    def cross(a, i):
        q = lax.rem(a, owned)
        return remote(
            slot(a, x, i, my_rows), slot(a, x, i, my_rows), x_send.at[q, i], x_recv.at[q, i], term=1 - x)

    def cross_in(q, i):
        a = x * owned + q
        return remote(
            slot(a, 1 - x, i, my_rows), slot(a, 1 - x, i, my_rows), x_send.at[q, i], x_recv.at[q, i], term=1 - x)

    def sibling(q, column, i):
        a = x * owned + q
        return remote(
            slot(a, column, i, my_rows), slot(a, column, i, my_rows),
            s_send.at[q, column, i], s_recv.at[q, column, i], half=1 - h)

    def sibling_in(q, column, i):
        a = x * owned + q
        return remote(
            slot(a, column, i, other_rows), slot(a, column, i, other_rows),
            s_send.at[q, column, i], s_recv.at[q, column, i], half=1 - h)

    def block_for(b, i, s):
        j = idx[b * capacity + x * share + i * STEP + s]
        block = psi[jnp.minimum(j, per_sector - 1)]
        return jnp.where(j < per_sector, block, jnp.zeros_like(block))

    def send(i):
        for d in range(n_block - 1, 0, -1):
            b = lax.rem(z + d, n_block)
            for s in range(STEP):
                stage[d - 1, i * STEP + s] = block_for(b, i, s)
            psi_out(d, i).start()
        for s in range(STEP):
            buf[z, x * share + i * STEP + s, my_rows, :] = block_for(z, i, s)

    def hand_on(a, i):
        @pl.when(a // owned == x)
        def _():
            sibling(lax.rem(a, owned), x, i).start()

        @pl.when(a // owned != x)
        def _():
            cross(a, i).start()

    def product(i):
        count = owned * 2 * STEP

        def one(j, carry):
            q, rest = j // (2 * STEP), lax.rem(j, 2 * STEP)
            k = (rest // STEP) * share + i * STEP + lax.rem(rest, STEP)
            a = x * owned + q
            got = jnp.dot(
                lall[a].reshape(terms * rows, width), buf[a, k], preferred_element_type=jnp.float32)
            for w in range(terms):
                mixed[pl.ds(pl.multiple_of(j * rows, rows), rows), w * width:(w + 1) * width] = (
                    got[w * rows:(w + 1) * rows].astype(jnp.bfloat16))
            return carry

        lax.fori_loop(0, count, one, 0)
        span = here * width
        total = None
        for g in range(2):
            part = jnp.dot(
                mixed[:, g * span:(g + 1) * span], rall[g * here:(g + 1) * here].reshape(span, width),
                preferred_element_type=jnp.float32).astype(jnp.bfloat16).astype(jnp.float32)
            total = part if total is None else total + part
        total = total.astype(jnp.bfloat16)
        for q in range(owned):
            for c in range(2):
                for s in range(STEP):
                    j = (q * 2 + c) * STEP + s
                    out[q * capacity + c * share + i * STEP + s] = total[j * rows:(j + 1) * rows]

    pl.semaphore_wait(barrier, n_block + 1)

    @pl.when(z < n_block - 1)
    def _():
        l_up(z, left).start()

    @pl.when(z > 0)
    def _():
        l_down(z, left).start()

    @pl.when(z // owned != x)
    def _():
        l_cross(z, left).start()

    r_cross().start()
    for i in range(AHEAD):
        send(i)
    lall[z, pl.ds(x * here, here)] = left[...]
    rall[pl.ds(x * here, here)] = right[...]
    r_cross_in().wait_recv()
    r_sibling().start()

    def step(i, carry):
        for d in range(1, n_block):
            @pl.when(i == d - 1)
            def _():
                pass_left(d)

        @pl.when(i + AHEAD < steps)
        def _():
            send(i + AHEAD)

        @pl.when(i < steps)
        def _():
            hand_on(z, i)
            for d in range(1, n_block):
                psi_in(d, i).wait_recv()
                hand_on(lax.rem(z + n_block - d, n_block), i)

        @pl.when((i >= 1) & (i <= steps))
        def _():
            for q in range(owned):
                cross_in(q, i - 1).wait_recv()
                sibling(q, 1 - x, i - 1).start()

        @pl.when(i == 2)
        def _():
            r_sibling_in().wait_recv()
            for q in range(owned):
                l_cross_in(q).wait_recv()

        @pl.when(i >= 2)
        def _():
            for q in range(owned):
                for c in range(2):
                    sibling_in(q, c, i - 2).wait_recv()
            product(i - 2)

        return carry

    lax.fori_loop(0, steps + 2, step, 0)

    for a in range(n_block):
        @pl.when((z < n_block - 1) & (a <= z))
        def _():
            l_up(a, l_part(a, x)).wait_send()

        @pl.when((z > 0) & (a >= z))
        def _():
            l_down(a, l_part(a, x)).wait_send()
    for q in range(owned):
        l_cross((1 - x) * owned + q, l_part((1 - x) * owned + q, x)).wait_send()
    r_cross().wait_send()
    r_sibling().wait_send()

    def drain(i, carry):
        for d in range(1, n_block):
            psi_out(d, i).wait_send()
        for q in range(owned):
            cross((1 - x) * owned + q, i).wait_send()
            for c in range(2):
                sibling(q, c, i).wait_send()
        return carry

    lax.fori_loop(0, steps, drain, 0)


def owner_computes(psi_blocks, left_env, right_env, right_owner):
    n_block = lax.axis_size("block")
    per_sector, rows, width = psi_blocks.shape
    capacity = max(2, 2 * per_sector // n_block)
    here = left_env.shape[0]
    owned = n_block // 2
    share = capacity // 2
    steps = share // STEP
    idx = slot_sources(right_owner, per_sector, n_block, capacity)
    dma = pltpu.SemaphoreType.DMA
    vmem = pl.BlockSpec(memory_space=pltpu.VMEM)
    return pl.pallas_call(
        functools.partial(kernel, n_block, capacity),
        out_shape=jax.ShapeDtypeStruct((owned * capacity, rows, width), jnp.bfloat16),
        in_specs=[pl.BlockSpec(memory_space=pltpu.SMEM), vmem, vmem, vmem],
        out_specs=vmem,
        scratch_shapes=[
            pltpu.VMEM((n_block - 1, share, rows, width), jnp.bfloat16),
            pltpu.VMEM((n_block, capacity, 2 * rows, width), jnp.bfloat16),
            pltpu.VMEM((n_block, 2 * here, rows, width), jnp.bfloat16),
            pltpu.VMEM((2 * here, width, width), jnp.bfloat16),
            pltpu.VMEM((owned * 2 * STEP * rows, 2 * here * width), jnp.bfloat16),
            dma((n_block - 1, steps)), dma((n_block - 1, steps)),
            dma((owned, steps)), dma((owned, steps)),
            dma((owned, 2, steps)), dma((owned, 2, steps)),
            dma((2, n_block)), dma((n_block,)),
            dma((owned,)), dma((owned,)),
            dma((2,)), dma((2,)),
        ],
        compiler_params=pltpu.CompilerParams(
            collective_id=0, has_side_effects=True, vmem_limit_bytes=48 * 2**20),
    )(idx, psi_blocks, left_env[:, 0], right_env[:, 0])


def exchanged(psi_blocks, left_env, right_env, right_owner):
    n_block = lax.axis_size("block")
    per_sector = psi_blocks.shape[0]
    capacity = max(2, 2 * per_sector // n_block)
    rows, width = psi_blocks.shape[1], psi_blocks.shape[2]
    here = left_env.shape[0]
    idx = slot_sources(right_owner, per_sector, n_block, capacity)
    dispatch = (
        idx[:, None] == jnp.arange(per_sector, dtype=jnp.int32)[None, :]
    ).astype(jnp.bfloat16)
    blended = jnp.einsum(
        "wik,bkc->wbic", left_env[:, 0],
        lax.all_gather(psi_blocks, "half", axis=1, tiled=True),
        preferred_element_type=jnp.float32,
    ).astype(jnp.bfloat16)
    outgoing = jnp.einsum(
        "sb,wbrc->wsrc", dispatch, blended, preferred_element_type=jnp.float32
    ).astype(jnp.bfloat16)
    outgoing = outgoing.reshape(here, n_block, capacity, rows, width)
    arrived = lax.all_to_all(outgoing, "block", split_axis=1, concat_axis=1, tiled=True)
    arrived = arrived.reshape(here, n_block * capacity, rows, width)
    partial_value = jnp.zeros((n_block * capacity, rows, width), jnp.float32)
    for w in range(here):
        partial_value = partial_value + jnp.einsum(
            "src,cn->srn", arrived[w], right_env[w, 0], preferred_element_type=jnp.float32)
    return lax.psum_scatter(
        partial_value.astype(jnp.bfloat16), "term", scatter_dimension=0, tiled=True)


def solution(mesh):
    in_specs = (
        P(("groups", "block"), "half", None),
        P(("groups", "term"), "block", "half", None),
        P(("groups", "term"), "block", None, None),
        P("groups", None),
    )
    out_specs = P(("groups", "block", "term"), "half", None)
    small = mesh.shape["term"] == 2 and mesh.shape["half"] == 2 and mesh.shape["block"] == 4
    body = owner_computes if small else exchanged
    return jax.shard_map(body, mesh=mesh, in_specs=in_specs, out_specs=out_specs, check_vma=False)
```

```python
import functools

import jax
import jax.numpy as jnp
from jax import lax
from jax.experimental import pallas as pl
from jax.experimental.pallas import tpu as pltpu
from jax.sharding import PartitionSpec as P

MESH = pl.DeviceIdType.MESH
STEP = 1
AHEAD = 4
FIRST = 1
LATE = 3


def slot_sources(right_owner, per_sector, n_block, capacity):
    source = lax.axis_index("block")
    targets = lax.dynamic_slice_in_dim(right_owner[:, 0], source * per_sector, per_sector)
    position = jnp.arange(per_sector, dtype=jnp.int32)
    upto = position[:, None] >= position[None, :]
    named = targets[None, :] == jnp.arange(n_block, dtype=jnp.int32)[:, None]
    count = jnp.sum((named[:, None, :] & upto[None]).astype(jnp.int32), axis=2)
    order = jnp.arange(capacity, dtype=jnp.int32)
    return jnp.sum((count[:, None, :] <= order[None, :, None]).astype(jnp.int32), axis=2).reshape(-1)


def kernel(
    n_block, capacity,
    idx, psi, left, right, out,
    psi_here, stage, buf, lall, rall, mixed, done,
    z_send, z_recv, x_send, x_recv, s_send, s_recv,
    lz_send, lz_recv, lx_send, lx_recv, r_send, r_recv, own_sem, out_sem,
):
    z, x, h = lax.axis_index("block"), lax.axis_index("term"), lax.axis_index("half")
    per_sector, rows, width = psi.shape
    here = left.shape[0]
    terms = 2 * here
    share = capacity // 2
    steps = share // STEP
    per_core = here // 2
    owned = n_block // 2

    def remote(src, dst, send, recv, **where):
        return pltpu.make_async_remote_copy(
            src_ref=src, dst_ref=dst, send_sem=send, recv_sem=recv,
            device_id=where, device_id_type=MESH,
        )

    own = [
        pltpu.make_async_copy(psi, psi_here, own_sem.at[0]),
        pltpu.make_async_copy(left, lall.at[z, pl.ds(x * here, here)], own_sem.at[1]),
        pltpu.make_async_copy(right, rall.at[pl.ds(x * here, here)], own_sem.at[2]),
    ]
    own[0].start()

    barrier = pltpu.get_barrier_semaphore()
    for d in range(1, n_block):
        pl.semaphore_signal(
            barrier, inc=1, device_id={"block": lax.rem(z + d, n_block)}, device_id_type=MESH)
    pl.semaphore_signal(barrier, inc=1, device_id={"term": 1 - x}, device_id_type=MESH)
    pl.semaphore_signal(barrier, inc=1, device_id={"half": 1 - h}, device_id_type=MESH)

    my_rows = pl.ds(pl.multiple_of(h * rows, rows), rows)
    other_rows = pl.ds(pl.multiple_of((1 - h) * rows, rows), rows)

    def slot(a, column, i, which):
        return buf.at[a, pl.ds(column * share + i * STEP, STEP), which, :]

    def l_part(a, column):
        return lall.at[a, pl.ds(column * here, here)]

    def l_up(a, src):
        return remote(src, l_part(a, x), lz_send.at[0, a], lz_recv.at[a], block=z + 1)

    def l_down(a, src):
        return remote(src, l_part(a, x), lz_send.at[1, a], lz_recv.at[a], block=z - 1)

    def l_cross(a, src):
        return remote(src, l_part(a, x), lx_send.at[lax.rem(a, owned)], lx_recv.at[lax.rem(a, owned)], term=1 - x)

    def l_cross_in(q):
        return remote(
            l_part(x * owned + q, 1 - x), l_part(x * owned + q, 1 - x), lx_send.at[q], lx_recv.at[q], term=1 - x)

    def pass_left(d):
        @pl.when(z - d >= 0)
        def _():
            a = z - d
            l_up(a, l_part(a, x)).wait_recv()

            @pl.when(z < n_block - 1)
            def _():
                l_up(a, l_part(a, x)).start()

            @pl.when(a // owned != x)
            def _():
                l_cross(a, l_part(a, x)).start()

        @pl.when(z + d < n_block)
        def _():
            a = z + d
            l_down(a, l_part(a, x)).wait_recv()

            @pl.when(z > 0)
            def _():
                l_down(a, l_part(a, x)).start()

            @pl.when(a // owned != x)
            def _():
                l_cross(a, l_part(a, x)).start()

    def r_part(column, core):
        return rall.at[pl.ds(column * here + core * per_core, per_core)]

    def r_cross():
        return remote(
            right.at[pl.ds(h * per_core, per_core)], r_part(x, h), r_send.at[0], r_recv.at[0], term=1 - x)

    def r_cross_in():
        return remote(r_part(1 - x, h), r_part(1 - x, h), r_send.at[0], r_recv.at[0], term=1 - x)

    def r_sibling():
        return remote(r_part(1 - x, h), r_part(1 - x, h), r_send.at[1], r_recv.at[1], half=1 - h)

    def r_sibling_in():
        return remote(r_part(1 - x, 1 - h), r_part(1 - x, 1 - h), r_send.at[1], r_recv.at[1], half=1 - h)

    def psi_out(d, i):
        b = lax.rem(z + d, n_block)
        return remote(
            stage.at[d - 1, pl.ds(i * STEP, STEP)], slot(z, x, i, my_rows),
            z_send.at[d - 1, i], z_recv.at[d - 1, i], block=b)

    def psi_in(d, i):
        a = lax.rem(z + n_block - d, n_block)
        return remote(
            stage.at[d - 1, pl.ds(i * STEP, STEP)], slot(a, x, i, my_rows),
            z_send.at[d - 1, i], z_recv.at[d - 1, i], block=a)

    def cross(a, i):
        q = lax.rem(a, owned)
        return remote(
            slot(a, x, i, my_rows), slot(a, x, i, my_rows), x_send.at[q, i], x_recv.at[q, i], term=1 - x)

    def cross_in(q, i):
        a = x * owned + q
        return remote(
            slot(a, 1 - x, i, my_rows), slot(a, 1 - x, i, my_rows), x_send.at[q, i], x_recv.at[q, i], term=1 - x)

    def sibling(q, column, i):
        a = x * owned + q
        return remote(
            slot(a, column, i, my_rows), slot(a, column, i, my_rows),
            s_send.at[q, column, i], s_recv.at[q, column, i], half=1 - h)

    def sibling_in(q, column, i):
        a = x * owned + q
        return remote(
            slot(a, column, i, other_rows), slot(a, column, i, other_rows),
            s_send.at[q, column, i], s_recv.at[q, column, i], half=1 - h)

    def block_for(b, i, s):
        j = idx[b * capacity + x * share + i * STEP + s]
        block = psi_here[jnp.minimum(j, per_sector - 1)]
        return jnp.where(j < per_sector, block, jnp.zeros_like(block))

    def send(i):
        for d in range(n_block - 1, 0, -1):
            b = lax.rem(z + d, n_block)
            for s in range(STEP):
                stage[d - 1, i * STEP + s] = block_for(b, i, s)
            psi_out(d, i).start()
        for s in range(STEP):
            buf[z, x * share + i * STEP + s, my_rows, :] = block_for(z, i, s)

    def hand_on(a, i):
        @pl.when(a // owned == x)
        def _():
            sibling(lax.rem(a, owned), x, i).start()

        @pl.when(a // owned != x)
        def _():
            cross(a, i).start()

    def result(q, column, i):
        at = pl.ds(q * capacity + column * share + i * STEP, STEP)
        return pltpu.make_async_copy(done.at[at], out.at[at], out_sem.at[q, column, i])

    def product(column, i):
        first = column * share + i * STEP
        for q in range(owned):
            sibling_in(q, column, i).wait_recv()

        def one(j, carry):
            q, s = j // STEP, lax.rem(j, STEP)
            got = jnp.dot(
                lall[x * owned + q].reshape(terms * rows, width), buf[x * owned + q, first + s],
                preferred_element_type=jnp.float32)
            for w in range(terms):
                mixed[pl.ds(pl.multiple_of(j * rows, rows), rows), w * width:(w + 1) * width] = (
                    got[w * rows:(w + 1) * rows].astype(jnp.bfloat16))
            return carry

        lax.fori_loop(0, owned * STEP, one, 0)
        span = here * width
        total = None
        for g in range(2):
            part = jnp.dot(
                mixed[:, g * span:(g + 1) * span], rall[g * here:(g + 1) * here].reshape(span, width),
                preferred_element_type=jnp.float32).astype(jnp.bfloat16).astype(jnp.float32)
            total = part if total is None else total + part
        total = total.astype(jnp.bfloat16)
        for q in range(owned):
            for s in range(STEP):
                j = q * STEP + s
                done[q * capacity + first + s] = total[j * rows:(j + 1) * rows]
            result(q, column, i).start()

    def products(column, i, arrived):
        def upto(t):
            most = jnp.minimum(arrived + t - i, steps)
            return jnp.where(t >= LATE, jnp.maximum(jnp.minimum(2 * (t - LATE) + 2, most), 0), 0)

        def whole(n, carry):
            product(column, n)
            return carry

        lax.fori_loop(upto(i - 1), upto(i), whole, 0)

    pl.semaphore_wait(barrier, n_block + 1)

    @pl.when(z < n_block - 1)
    def _():
        l_up(z, left).start()

    @pl.when(z > 0)
    def _():
        l_down(z, left).start()

    @pl.when(z // owned != x)
    def _():
        l_cross(z, left).start()

    r_cross().start()
    own[0].wait()
    own[1].start()
    own[2].start()
    for i in range(FIRST):
        send(i)
    r_cross_in().wait_recv()
    r_sibling().start()

    for d in range(1, n_block):
        pass_left(d)
        if FIRST + d <= AHEAD:
            send(FIRST + d - 1)
    for i in range(FIRST + n_block - 1, AHEAD):
        send(i)

    def step(i, carry):
        @pl.when(i + AHEAD < steps)
        def _():
            send(i + AHEAD)

        @pl.when(i < steps)
        def _():
            hand_on(z, i)
            for d in range(1, n_block):
                psi_in(d, i).wait_recv()
                hand_on(lax.rem(z + n_block - d, n_block), i)

        @pl.when(i == LATE)
        def _():
            own[1].wait()
            own[2].wait()
            r_sibling_in().wait_recv()
            for q in range(owned):
                l_cross_in(q).wait_recv()

        products(x, i, i)

        @pl.when((i >= 1) & (i <= steps))
        def _():
            for q in range(owned):
                cross_in(q, i - 1).wait_recv()
                sibling(q, 1 - x, i - 1).start()

        products(1 - x, i, i - 1)
        return carry

    lax.fori_loop(0, steps + 2, step, 0)

    for a in range(n_block):
        @pl.when((z < n_block - 1) & (a <= z))
        def _():
            l_up(a, l_part(a, x)).wait_send()

        @pl.when((z > 0) & (a >= z))
        def _():
            l_down(a, l_part(a, x)).wait_send()
    for q in range(owned):
        l_cross((1 - x) * owned + q, l_part((1 - x) * owned + q, x)).wait_send()
    r_cross().wait_send()
    r_sibling().wait_send()

    def drain(i, carry):
        for d in range(1, n_block):
            psi_out(d, i).wait_send()
        for q in range(owned):
            cross((1 - x) * owned + q, i).wait_send()
            for c in range(2):
                sibling(q, c, i).wait_send()
                result(q, c, i).wait()
        return carry

    lax.fori_loop(0, steps, drain, 0)


def owner_computes(psi_blocks, left_env, right_env, right_owner):
    n_block = lax.axis_size("block")
    per_sector, rows, width = psi_blocks.shape
    capacity = max(2, 2 * per_sector // n_block)
    here = left_env.shape[0]
    owned = n_block // 2
    share = capacity // 2
    steps = share // STEP
    idx = slot_sources(right_owner, per_sector, n_block, capacity)
    dma = pltpu.SemaphoreType.DMA
    anywhere = pl.BlockSpec(memory_space=pl.ANY)
    return pl.pallas_call(
        functools.partial(kernel, n_block, capacity),
        out_shape=jax.ShapeDtypeStruct((owned * capacity, rows, width), jnp.bfloat16),
        in_specs=[pl.BlockSpec(memory_space=pltpu.SMEM), anywhere, anywhere, anywhere],
        out_specs=anywhere,
        scratch_shapes=[
            pltpu.VMEM((per_sector, rows, width), jnp.bfloat16),
            pltpu.VMEM((n_block - 1, share, rows, width), jnp.bfloat16),
            pltpu.VMEM((n_block, capacity, 2 * rows, width), jnp.bfloat16),
            pltpu.VMEM((n_block, 2 * here, rows, width), jnp.bfloat16),
            pltpu.VMEM((2 * here, width, width), jnp.bfloat16),
            pltpu.VMEM((owned * STEP * rows, 2 * here * width), jnp.bfloat16),
            pltpu.VMEM((owned * capacity, rows, width), jnp.bfloat16),
            dma((n_block - 1, steps)), dma((n_block - 1, steps)),
            dma((owned, steps)), dma((owned, steps)),
            dma((owned, 2, steps)), dma((owned, 2, steps)),
            dma((2, n_block)), dma((n_block,)),
            dma((owned,)), dma((owned,)),
            dma((2,)), dma((2,)),
            dma((3,)), dma((owned, 2, steps)),
        ],
        compiler_params=pltpu.CompilerParams(
            collective_id=0, has_side_effects=True, vmem_limit_bytes=60 * 2**20),
    )(idx, psi_blocks, left_env[:, 0], right_env[:, 0])


def exchanged(psi_blocks, left_env, right_env, right_owner):
    n_block = lax.axis_size("block")
    per_sector = psi_blocks.shape[0]
    capacity = max(2, 2 * per_sector // n_block)
    rows, width = psi_blocks.shape[1], psi_blocks.shape[2]
    here = left_env.shape[0]
    idx = slot_sources(right_owner, per_sector, n_block, capacity)
    dispatch = (
        idx[:, None] == jnp.arange(per_sector, dtype=jnp.int32)[None, :]
    ).astype(jnp.bfloat16)
    blended = jnp.einsum(
        "wik,bkc->wbic", left_env[:, 0],
        lax.all_gather(psi_blocks, "half", axis=1, tiled=True),
        preferred_element_type=jnp.float32,
    ).astype(jnp.bfloat16)
    outgoing = jnp.einsum(
        "sb,wbrc->wsrc", dispatch, blended, preferred_element_type=jnp.float32
    ).astype(jnp.bfloat16)
    outgoing = outgoing.reshape(here, n_block, capacity, rows, width)
    arrived = lax.all_to_all(outgoing, "block", split_axis=1, concat_axis=1, tiled=True)
    arrived = arrived.reshape(here, n_block * capacity, rows, width)
    partial_value = jnp.zeros((n_block * capacity, rows, width), jnp.float32)
    for w in range(here):
        partial_value = partial_value + jnp.einsum(
            "src,cn->srn", arrived[w], right_env[w, 0], preferred_element_type=jnp.float32)
    return lax.psum_scatter(
        partial_value.astype(jnp.bfloat16), "term", scatter_dimension=0, tiled=True)


def solution(mesh):
    in_specs = (
        P(("groups", "block"), "half", None),
        P(("groups", "term"), "block", "half", None),
        P(("groups", "term"), "block", None, None),
        P("groups", None),
    )
    out_specs = P(("groups", "block", "term"), "half", None)
    small = mesh.shape["term"] == 2 and mesh.shape["half"] == 2 and mesh.shape["block"] == 4
    body = owner_computes if small else exchanged
    return jax.shard_map(body, mesh=mesh, in_specs=in_specs, out_specs=out_specs, check_vma=False)
```

```python
import functools

import jax
import jax.numpy as jnp
from jax import lax
from jax.experimental import pallas as pl
from jax.experimental.pallas import tpu as pltpu
from jax.sharding import PartitionSpec as P

MESH = pl.DeviceIdType.MESH
STEP = 1
AHEAD = 5
FIRST = 1
PIECES = 4
LATE = 3


def slot_sources(right_owner, per_sector, n_block, capacity):
    source = lax.axis_index("block")
    targets = lax.dynamic_slice_in_dim(right_owner[:, 0], source * per_sector, per_sector)
    position = jnp.arange(per_sector, dtype=jnp.int32)
    upto = position[:, None] >= position[None, :]
    named = targets[None, :] == jnp.arange(n_block, dtype=jnp.int32)[:, None]
    count = jnp.sum((named[:, None, :] & upto[None]).astype(jnp.int32), axis=2)
    order = jnp.arange(capacity, dtype=jnp.int32)
    return jnp.sum((count[:, None, :] <= order[None, :, None]).astype(jnp.int32), axis=2).reshape(-1)


def kernel(
    n_block, capacity,
    idx, psi, left, right, out,
    psi_here, stage, buf, lall, rall, mixed,
    z_send, z_recv, x_send, x_recv, s_send, s_recv,
    lz_send, lz_recv, lx_send, lx_recv, r_send, r_recv, own_sem,
):
    z, x, h = lax.axis_index("block"), lax.axis_index("term"), lax.axis_index("half")
    per_sector, rows, width = psi.shape
    here = left.shape[0]
    terms = 2 * here
    share = capacity // 2
    steps = share // STEP
    per_core = here // 2
    owned = n_block // 2

    def remote(src, dst, send, recv, **where):
        return pltpu.make_async_remote_copy(
            src_ref=src, dst_ref=dst, send_sem=send, recv_sem=recv,
            device_id=where, device_id_type=MESH,
        )

    own = [
        pltpu.make_async_copy(psi, psi_here, own_sem.at[0]),
        pltpu.make_async_copy(left, lall.at[z, pl.ds(x * here, here)], own_sem.at[1]),
        pltpu.make_async_copy(right, rall.at[pl.ds(x * here, here)], own_sem.at[2]),
    ]
    own[0].start()

    barrier = pltpu.get_barrier_semaphore()
    for d in range(1, n_block):
        pl.semaphore_signal(
            barrier, inc=1, device_id={"block": lax.rem(z + d, n_block)}, device_id_type=MESH)
    pl.semaphore_signal(barrier, inc=1, device_id={"term": 1 - x}, device_id_type=MESH)
    pl.semaphore_signal(barrier, inc=1, device_id={"half": 1 - h}, device_id_type=MESH)

    my_rows = pl.ds(pl.multiple_of(h * rows, rows), rows)
    other_rows = pl.ds(pl.multiple_of((1 - h) * rows, rows), rows)

    def slot(a, column, i, which):
        return buf.at[a, pl.ds(column * share + i * STEP, STEP), which, :]

    part = here // PIECES

    def l_part(a, column, p):
        return lall.at[a, pl.ds(column * here + p * part, part)]

    def l_own(p):
        return left.at[pl.ds(p * part, part)]

    def l_up(a, p, src):
        return remote(src, l_part(a, x, p), lz_send.at[0, a, p], lz_recv.at[a, p], block=z + 1)

    def l_down(a, p, src):
        return remote(src, l_part(a, x, p), lz_send.at[1, a, p], lz_recv.at[a, p], block=z - 1)

    def l_cross(a, p, src):
        q = lax.rem(a, owned)
        return remote(src, l_part(a, x, p), lx_send.at[q, p], lx_recv.at[q, p], term=1 - x)

    def l_cross_in(q, p):
        a = x * owned + q
        return remote(
            l_part(a, 1 - x, p), l_part(a, 1 - x, p), lx_send.at[q, p], lx_recv.at[q, p], term=1 - x)

    def pass_left(d, p):
        @pl.when(z - d >= 0)
        def _():
            a = z - d
            l_up(a, p, l_part(a, x, p)).wait_recv()

            @pl.when(z < n_block - 1)
            def _():
                l_up(a, p, l_part(a, x, p)).start()

            @pl.when(a // owned != x)
            def _():
                l_cross(a, p, l_part(a, x, p)).start()

        @pl.when(z + d < n_block)
        def _():
            a = z + d
            l_down(a, p, l_part(a, x, p)).wait_recv()

            @pl.when(z > 0)
            def _():
                l_down(a, p, l_part(a, x, p)).start()

            @pl.when(a // owned != x)
            def _():
                l_cross(a, p, l_part(a, x, p)).start()

    def r_part(column, core):
        return rall.at[pl.ds(column * here + core * per_core, per_core)]

    def r_cross():
        return remote(
            right.at[pl.ds(h * per_core, per_core)], r_part(x, h), r_send.at[0], r_recv.at[0], term=1 - x)

    def r_cross_in():
        return remote(r_part(1 - x, h), r_part(1 - x, h), r_send.at[0], r_recv.at[0], term=1 - x)

    def r_sibling():
        return remote(r_part(1 - x, h), r_part(1 - x, h), r_send.at[1], r_recv.at[1], half=1 - h)

    def r_sibling_in():
        return remote(r_part(1 - x, 1 - h), r_part(1 - x, 1 - h), r_send.at[1], r_recv.at[1], half=1 - h)

    def psi_out(d, i):
        b = lax.rem(z + d, n_block)
        return remote(
            stage.at[d - 1, pl.ds(i * STEP, STEP)], slot(z, x, i, my_rows),
            z_send.at[d - 1, i], z_recv.at[d - 1, i], block=b)

    def psi_in(d, i):
        a = lax.rem(z + n_block - d, n_block)
        return remote(
            stage.at[d - 1, pl.ds(i * STEP, STEP)], slot(a, x, i, my_rows),
            z_send.at[d - 1, i], z_recv.at[d - 1, i], block=a)

    def cross(a, i):
        q = lax.rem(a, owned)
        return remote(
            slot(a, x, i, my_rows), slot(a, x, i, my_rows), x_send.at[q, i], x_recv.at[q, i], term=1 - x)

    def cross_in(q, i):
        a = x * owned + q
        return remote(
            slot(a, 1 - x, i, my_rows), slot(a, 1 - x, i, my_rows), x_send.at[q, i], x_recv.at[q, i], term=1 - x)

    def sibling(q, column, i):
        a = x * owned + q
        return remote(
            slot(a, column, i, my_rows), slot(a, column, i, my_rows),
            s_send.at[q, column, i], s_recv.at[q, column, i], half=1 - h)

    def sibling_in(q, column, i):
        a = x * owned + q
        return remote(
            slot(a, column, i, other_rows), slot(a, column, i, other_rows),
            s_send.at[q, column, i], s_recv.at[q, column, i], half=1 - h)

    def block_for(b, i, s):
        j = idx[b * capacity + x * share + i * STEP + s]
        block = psi_here[jnp.minimum(j, per_sector - 1)]
        return jnp.where(j < per_sector, block, jnp.zeros_like(block))

    def send(i):
        for d in range(1, n_block):
            b = lax.rem(z + d, n_block)
            for s in range(STEP):
                stage[d - 1, i * STEP + s] = block_for(b, i, s)
            psi_out(d, i).start()
        for s in range(STEP):
            buf[z, x * share + i * STEP + s, my_rows, :] = block_for(z, i, s)

    def hand_on(a, i):
        @pl.when(a // owned == x)
        def _():
            sibling(lax.rem(a, owned), x, i).start()

        @pl.when(a // owned != x)
        def _():
            cross(a, i).start()

    def product(column, i):
        first = column * share + i * STEP
        for q in range(owned):
            sibling_in(q, column, i).wait_recv()

        def one(j, carry):
            q, s = j // STEP, lax.rem(j, STEP)
            got = jnp.dot(
                lall[x * owned + q].reshape(terms * rows, width), buf[x * owned + q, first + s],
                preferred_element_type=jnp.float32)
            for w in range(terms):
                mixed[pl.ds(pl.multiple_of(j * rows, rows), rows), w * width:(w + 1) * width] = (
                    got[w * rows:(w + 1) * rows].astype(jnp.bfloat16))
            return carry

        lax.fori_loop(0, owned * STEP, one, 0)
        span = here * width
        total = None
        for g in range(2):
            part = jnp.dot(
                mixed[:, g * span:(g + 1) * span], rall[g * here:(g + 1) * here].reshape(span, width),
                preferred_element_type=jnp.float32).astype(jnp.bfloat16).astype(jnp.float32)
            total = part if total is None else total + part
        total = total.astype(jnp.bfloat16)
        for q in range(owned):
            for s in range(STEP):
                j = q * STEP + s
                out[q * capacity + first + s] = total[j * rows:(j + 1) * rows]

    def products(column, i, arrived):
        def upto(t):
            most = jnp.minimum(arrived + t - i, steps)
            return jnp.where(t >= LATE, jnp.maximum(jnp.minimum(2 * (t - LATE) + 2, most), 0), 0)

        def whole(n, carry):
            product(column, n)
            return carry

        lax.fori_loop(upto(i - 1), upto(i), whole, 0)

    pl.semaphore_wait(barrier, n_block + 1)

    for p in range(PIECES):
        @pl.when(z < n_block - 1)
        def _():
            l_up(z, p, l_own(p)).start()

        @pl.when(z > 0)
        def _():
            l_down(z, p, l_own(p)).start()

        @pl.when(z // owned != x)
        def _():
            l_cross(z, p, l_own(p)).start()

    r_cross().start()
    own[0].wait()
    own[1].start()
    own[2].start()
    for i in range(FIRST):
        send(i)
    r_cross_in().wait_recv()
    r_sibling().start()

    for d in range(1, n_block):
        for p in range(PIECES):
            pass_left(d, p)
        if FIRST + d <= AHEAD:
            send(FIRST + d - 1)
    for i in range(FIRST + n_block - 1, AHEAD):
        send(i)

    def step(i, carry):
        @pl.when(i + AHEAD < steps)
        def _():
            send(i + AHEAD)

        @pl.when(i < steps)
        def _():
            hand_on(z, i)
            for d in range(1, n_block):
                psi_in(d, i).wait_recv()
                hand_on(lax.rem(z + n_block - d, n_block), i)

        @pl.when(i == LATE)
        def _():
            own[1].wait()
            own[2].wait()
            r_sibling_in().wait_recv()
            for q in range(owned):
                for p in range(PIECES):
                    l_cross_in(q, p).wait_recv()

        products(x, i, i)

        @pl.when((i >= 1) & (i <= steps))
        def _():
            for q in range(owned):
                cross_in(q, i - 1).wait_recv()
                sibling(q, 1 - x, i - 1).start()

        products(1 - x, i, i - 1)
        return carry

    lax.fori_loop(0, steps + 2, step, 0)

    for p in range(PIECES):
        for a in range(n_block):
            @pl.when((z < n_block - 1) & (a <= z))
            def _():
                l_up(a, p, l_part(a, x, p)).wait_send()

            @pl.when((z > 0) & (a >= z))
            def _():
                l_down(a, p, l_part(a, x, p)).wait_send()
        for q in range(owned):
            a = (1 - x) * owned + q
            l_cross(a, p, l_part(a, x, p)).wait_send()
    r_cross().wait_send()
    r_sibling().wait_send()

    def drain(i, carry):
        for d in range(1, n_block):
            psi_out(d, i).wait_send()
        for q in range(owned):
            cross((1 - x) * owned + q, i).wait_send()
            for c in range(2):
                sibling(q, c, i).wait_send()
        return carry

    lax.fori_loop(0, steps, drain, 0)


def owner_computes(psi_blocks, left_env, right_env, right_owner):
    n_block = lax.axis_size("block")
    per_sector, rows, width = psi_blocks.shape
    capacity = max(2, 2 * per_sector // n_block)
    here = left_env.shape[0]
    owned = n_block // 2
    share = capacity // 2
    steps = share // STEP
    idx = slot_sources(right_owner, per_sector, n_block, capacity)
    dma = pltpu.SemaphoreType.DMA
    hbm = pl.BlockSpec(memory_space=pltpu.HBM)
    return pl.pallas_call(
        functools.partial(kernel, n_block, capacity),
        out_shape=jax.ShapeDtypeStruct((owned * capacity, rows, width), jnp.bfloat16),
        in_specs=[pl.BlockSpec(memory_space=pltpu.SMEM), hbm, hbm, hbm],
        out_specs=pl.BlockSpec(memory_space=pltpu.VMEM),
        scratch_shapes=[
            pltpu.VMEM((per_sector, rows, width), jnp.bfloat16),
            pltpu.VMEM((n_block - 1, share, rows, width), jnp.bfloat16),
            pltpu.VMEM((n_block, capacity, 2 * rows, width), jnp.bfloat16),
            pltpu.VMEM((n_block, 2 * here, rows, width), jnp.bfloat16),
            pltpu.VMEM((2 * here, width, width), jnp.bfloat16),
            pltpu.VMEM((owned * STEP * rows, 2 * here * width), jnp.bfloat16),
            dma((n_block - 1, steps)), dma((n_block - 1, steps)),
            dma((owned, steps)), dma((owned, steps)),
            dma((owned, 2, steps)), dma((owned, 2, steps)),
            dma((2, n_block, PIECES)), dma((n_block, PIECES)),
            dma((owned, PIECES)), dma((owned, PIECES)),
            dma((2,)), dma((2,)),
            dma((3,)),
        ],
        compiler_params=pltpu.CompilerParams(
            collective_id=0, has_side_effects=True, vmem_limit_bytes=36 * 2**20),
    )(idx, psi_blocks, left_env[:, 0], right_env[:, 0])


def exchanged(psi_blocks, left_env, right_env, right_owner):
    n_block = lax.axis_size("block")
    per_sector = psi_blocks.shape[0]
    capacity = max(2, 2 * per_sector // n_block)
    rows, width = psi_blocks.shape[1], psi_blocks.shape[2]
    here = left_env.shape[0]
    idx = slot_sources(right_owner, per_sector, n_block, capacity)
    dispatch = (
        idx[:, None] == jnp.arange(per_sector, dtype=jnp.int32)[None, :]
    ).astype(jnp.bfloat16)
    blended = jnp.einsum(
        "wik,bkc->wbic", left_env[:, 0],
        lax.all_gather(psi_blocks, "half", axis=1, tiled=True),
        preferred_element_type=jnp.float32,
    ).astype(jnp.bfloat16)
    outgoing = jnp.einsum(
        "sb,wbrc->wsrc", dispatch, blended, preferred_element_type=jnp.float32
    ).astype(jnp.bfloat16)
    outgoing = outgoing.reshape(here, n_block, capacity, rows, width)
    arrived = lax.all_to_all(outgoing, "block", split_axis=1, concat_axis=1, tiled=True)
    arrived = arrived.reshape(here, n_block * capacity, rows, width)
    partial_value = jnp.zeros((n_block * capacity, rows, width), jnp.float32)
    for w in range(here):
        partial_value = partial_value + jnp.einsum(
            "src,cn->srn", arrived[w], right_env[w, 0], preferred_element_type=jnp.float32)
    return lax.psum_scatter(
        partial_value.astype(jnp.bfloat16), "term", scatter_dimension=0, tiled=True)


def solution(mesh):
    in_specs = (
        P(("groups", "block"), "half", None),
        P(("groups", "term"), "block", "half", None),
        P(("groups", "term"), "block", None, None),
        P("groups", None),
    )
    out_specs = P(("groups", "block", "term"), "half", None)
    small = mesh.shape["term"] == 2 and mesh.shape["half"] == 2 and mesh.shape["block"] == 4
    body = owner_computes if small else exchanged
    return jax.shard_map(body, mesh=mesh, in_specs=in_specs, out_specs=out_specs, check_vma=False)
```

```python
import functools

import jax
import jax.numpy as jnp
from jax import lax
from jax.experimental import pallas as pl
from jax.experimental.pallas import tpu as pltpu
from jax.sharding import PartitionSpec as P

MESH = pl.DeviceIdType.MESH
STEP = 1
AHEAD = 5
FIRST = 1
PIECES = 4
LATE = 3


def slot_sources(right_owner, per_sector, n_block, capacity):
    source = lax.axis_index("block")
    targets = lax.dynamic_slice_in_dim(right_owner[:, 0], source * per_sector, per_sector)
    position = jnp.arange(per_sector, dtype=jnp.int32)
    upto = position[:, None] >= position[None, :]
    named = targets[None, :] == jnp.arange(n_block, dtype=jnp.int32)[:, None]
    count = jnp.sum((named[:, None, :] & upto[None]).astype(jnp.int32), axis=2)
    order = jnp.arange(capacity, dtype=jnp.int32)
    return jnp.sum((count[:, None, :] <= order[None, :, None]).astype(jnp.int32), axis=2).reshape(-1)


def kernel(
    n_block, capacity,
    idx, psi, left, right, out,
    psi_here, stage, buf, lall, rall, mixed,
    z_send, z_recv, x_send, x_recv, s_send, s_recv,
    lz_send, lz_recv, lx_send, lx_recv, r_send, r_recv, own_sem,
):
    z, x, h = lax.axis_index("block"), lax.axis_index("term"), lax.axis_index("half")
    per_sector, rows, width = psi.shape
    here = left.shape[0]
    terms = 2 * here
    share = capacity // 2
    steps = share // STEP
    per_core = here // 2
    owned = n_block // 2

    def remote(src, dst, send, recv, **where):
        return pltpu.make_async_remote_copy(
            src_ref=src, dst_ref=dst, send_sem=send, recv_sem=recv,
            device_id=where, device_id_type=MESH,
        )

    own = [
        pltpu.make_async_copy(psi, psi_here, own_sem.at[0]),
        pltpu.make_async_copy(left, lall.at[z, pl.ds(x * here, here)], own_sem.at[1]),
        pltpu.make_async_copy(right, rall.at[pl.ds(x * here, here)], own_sem.at[2]),
    ]
    own[0].start()

    barrier = pltpu.get_barrier_semaphore()
    for d in range(1, n_block):
        pl.semaphore_signal(
            barrier, inc=1, device_id={"block": lax.rem(z + d, n_block)}, device_id_type=MESH)
    pl.semaphore_signal(barrier, inc=1, device_id={"term": 1 - x}, device_id_type=MESH)
    pl.semaphore_signal(barrier, inc=1, device_id={"half": 1 - h}, device_id_type=MESH)

    my_rows = pl.ds(pl.multiple_of(h * rows, rows), rows)
    other_rows = pl.ds(pl.multiple_of((1 - h) * rows, rows), rows)

    def slot(a, column, i, which):
        return buf.at[a, pl.ds(column * share + i * STEP, STEP), which, :]

    part = here // PIECES

    def l_part(a, column, p):
        return lall.at[a, pl.ds(column * here + p * part, part)]

    def l_own(p):
        return left.at[pl.ds(p * part, part)]

    def l_up(a, p, src):
        return remote(src, l_part(a, x, p), lz_send.at[0, a, p], lz_recv.at[a, p], block=z + 1)

    def l_down(a, p, src):
        return remote(src, l_part(a, x, p), lz_send.at[1, a, p], lz_recv.at[a, p], block=z - 1)

    def l_cross(a, p, src):
        q = lax.rem(a, owned)
        return remote(src, l_part(a, x, p), lx_send.at[q, p], lx_recv.at[q, p], term=1 - x)

    def l_cross_in(q, p):
        a = x * owned + q
        return remote(
            l_part(a, 1 - x, p), l_part(a, 1 - x, p), lx_send.at[q, p], lx_recv.at[q, p], term=1 - x)

    def pass_left(d, p):
        @pl.when(z - d >= 0)
        def _():
            a = z - d
            l_up(a, p, l_part(a, x, p)).wait_recv()

            @pl.when(z < n_block - 1)
            def _():
                l_up(a, p, l_part(a, x, p)).start()

            @pl.when(a // owned != x)
            def _():
                l_cross(a, p, l_part(a, x, p)).start()

        @pl.when(z + d < n_block)
        def _():
            a = z + d
            l_down(a, p, l_part(a, x, p)).wait_recv()

            @pl.when(z > 0)
            def _():
                l_down(a, p, l_part(a, x, p)).start()

            @pl.when(a // owned != x)
            def _():
                l_cross(a, p, l_part(a, x, p)).start()

    def r_part(column, core):
        return rall.at[pl.ds(column * here + core * per_core, per_core)]

    def r_cross():
        return remote(
            right.at[pl.ds(h * per_core, per_core)], r_part(x, h), r_send.at[0], r_recv.at[0], term=1 - x)

    def r_cross_in():
        return remote(r_part(1 - x, h), r_part(1 - x, h), r_send.at[0], r_recv.at[0], term=1 - x)

    def r_sibling():
        return remote(r_part(1 - x, h), r_part(1 - x, h), r_send.at[1], r_recv.at[1], half=1 - h)

    def r_sibling_in():
        return remote(r_part(1 - x, 1 - h), r_part(1 - x, 1 - h), r_send.at[1], r_recv.at[1], half=1 - h)

    def psi_out(d, i):
        b = lax.rem(z + d, n_block)
        return remote(
            stage.at[d - 1, pl.ds(i * STEP, STEP)], slot(z, x, i, my_rows),
            z_send.at[d - 1, i], z_recv.at[d - 1, i], block=b)

    def psi_in(d, i):
        a = lax.rem(z + n_block - d, n_block)
        return remote(
            stage.at[d - 1, pl.ds(i * STEP, STEP)], slot(a, x, i, my_rows),
            z_send.at[d - 1, i], z_recv.at[d - 1, i], block=a)

    def cross(a, i):
        q = lax.rem(a, owned)
        return remote(
            slot(a, x, i, my_rows), slot(a, x, i, my_rows), x_send.at[q, i], x_recv.at[q, i], term=1 - x)

    def cross_in(q, i):
        a = x * owned + q
        return remote(
            slot(a, 1 - x, i, my_rows), slot(a, 1 - x, i, my_rows), x_send.at[q, i], x_recv.at[q, i], term=1 - x)

    def sibling(q, column, i):
        a = x * owned + q
        return remote(
            slot(a, column, i, my_rows), slot(a, column, i, my_rows),
            s_send.at[q, column, i], s_recv.at[q, column, i], half=1 - h)

    def sibling_in(q, column, i):
        a = x * owned + q
        return remote(
            slot(a, column, i, other_rows), slot(a, column, i, other_rows),
            s_send.at[q, column, i], s_recv.at[q, column, i], half=1 - h)

    def block_for(b, i, s):
        j = idx[b * capacity + x * share + i * STEP + s]
        block = psi_here[jnp.minimum(j, per_sector - 1)]
        return jnp.where(j < per_sector, block, jnp.zeros_like(block))

    def send(i):
        for d in range(1, n_block):
            b = lax.rem(z + d, n_block)
            for s in range(STEP):
                stage[d - 1, i * STEP + s] = block_for(b, i, s)
            psi_out(d, i).start()
        for s in range(STEP):
            buf[z, x * share + i * STEP + s, my_rows, :] = block_for(z, i, s)

    def hand_on(a, i):
        @pl.when(a // owned == x)
        def _():
            sibling(lax.rem(a, owned), x, i).start()

        @pl.when(a // owned != x)
        def _():
            cross(a, i).start()

    def product(column, i):
        first = column * share + i * STEP
        for q in range(owned):
            sibling_in(q, column, i).wait_recv()

        def one(j, carry):
            q, s = j // STEP, lax.rem(j, STEP)
            got = jnp.dot(
                lall[x * owned + q].reshape(terms * rows, width), buf[x * owned + q, first + s],
                preferred_element_type=jnp.float32)
            for w in range(terms):
                mixed[pl.ds(pl.multiple_of(j * rows, rows), rows), w * width:(w + 1) * width] = (
                    got[w * rows:(w + 1) * rows].astype(jnp.bfloat16))
            return carry

        lax.fori_loop(0, owned * STEP, one, 0)
        span = here * width
        total = None
        for g in range(2):
            part = jnp.dot(
                mixed[:, g * span:(g + 1) * span], rall[g * here:(g + 1) * here].reshape(span, width),
                preferred_element_type=jnp.float32).astype(jnp.bfloat16).astype(jnp.float32)
            total = part if total is None else total + part
        total = total.astype(jnp.bfloat16)
        for q in range(owned):
            for s in range(STEP):
                j = q * STEP + s
                out[q * capacity + first + s] = total[j * rows:(j + 1) * rows]

    def products(column, i, arrived):
        def upto(t):
            most = jnp.minimum(arrived + t - i, steps)
            return jnp.where(t >= LATE, jnp.maximum(jnp.minimum(2 * (t - LATE) + 2, most), 0), 0)

        def whole(n, carry):
            product(column, n)
            return carry

        lax.fori_loop(upto(i - 1), upto(i), whole, 0)

    pl.semaphore_wait(barrier, n_block + 1)

    for p in range(PIECES):
        @pl.when(z < n_block - 1)
        def _():
            l_up(z, p, l_own(p)).start()

        @pl.when(z > 0)
        def _():
            l_down(z, p, l_own(p)).start()

        @pl.when(z // owned != x)
        def _():
            l_cross(z, p, l_own(p)).start()

    r_cross().start()
    own[0].wait()
    own[1].start()
    own[2].start()
    for i in range(FIRST):
        send(i)
    r_cross_in().wait_recv()
    r_sibling().start()

    for d in range(1, n_block):
        if FIRST + d <= AHEAD and d > 1:
            send(FIRST + d - 2)
        for p in range(PIECES):
            pass_left(d, p)
    for i in range(FIRST + n_block - 2, AHEAD):
        send(i)

    def step(i, carry):
        @pl.when(i + AHEAD < steps)
        def _():
            send(i + AHEAD)

        @pl.when(i < steps)
        def _():
            hand_on(z, i)
            for d in range(1, n_block):
                psi_in(d, i).wait_recv()
                hand_on(lax.rem(z + n_block - d, n_block), i)

        @pl.when(i == LATE)
        def _():
            own[1].wait()
            own[2].wait()
            r_sibling_in().wait_recv()
            for q in range(owned):
                for p in range(PIECES):
                    l_cross_in(q, p).wait_recv()

        products(x, i, i)

        @pl.when((i >= 1) & (i <= steps))
        def _():
            for q in range(owned):
                cross_in(q, i - 1).wait_recv()
                sibling(q, 1 - x, i - 1).start()

        products(1 - x, i, i - 1)
        return carry

    lax.fori_loop(0, steps + 2, step, 0)

    for p in range(PIECES):
        for a in range(n_block):
            @pl.when((z < n_block - 1) & (a <= z))
            def _():
                l_up(a, p, l_part(a, x, p)).wait_send()

            @pl.when((z > 0) & (a >= z))
            def _():
                l_down(a, p, l_part(a, x, p)).wait_send()
        for q in range(owned):
            a = (1 - x) * owned + q
            l_cross(a, p, l_part(a, x, p)).wait_send()
    r_cross().wait_send()
    r_sibling().wait_send()

    def drain(i, carry):
        for d in range(1, n_block):
            psi_out(d, i).wait_send()
        for q in range(owned):
            cross((1 - x) * owned + q, i).wait_send()
            for c in range(2):
                sibling(q, c, i).wait_send()
        return carry

    lax.fori_loop(0, steps, drain, 0)


def owner_computes(psi_blocks, left_env, right_env, right_owner):
    n_block = lax.axis_size("block")
    per_sector, rows, width = psi_blocks.shape
    capacity = max(2, 2 * per_sector // n_block)
    here = left_env.shape[0]
    owned = n_block // 2
    share = capacity // 2
    steps = share // STEP
    idx = slot_sources(right_owner, per_sector, n_block, capacity)
    dma = pltpu.SemaphoreType.DMA
    hbm = pl.BlockSpec(memory_space=pltpu.HBM)
    return pl.pallas_call(
        functools.partial(kernel, n_block, capacity),
        out_shape=jax.ShapeDtypeStruct((owned * capacity, rows, width), jnp.bfloat16),
        in_specs=[pl.BlockSpec(memory_space=pltpu.SMEM), hbm, hbm, hbm],
        out_specs=pl.BlockSpec(memory_space=pltpu.VMEM),
        scratch_shapes=[
            pltpu.VMEM((per_sector, rows, width), jnp.bfloat16),
            pltpu.VMEM((n_block - 1, share, rows, width), jnp.bfloat16),
            pltpu.VMEM((n_block, capacity, 2 * rows, width), jnp.bfloat16),
            pltpu.VMEM((n_block, 2 * here, rows, width), jnp.bfloat16),
            pltpu.VMEM((2 * here, width, width), jnp.bfloat16),
            pltpu.VMEM((owned * STEP * rows, 2 * here * width), jnp.bfloat16),
            dma((n_block - 1, steps)), dma((n_block - 1, steps)),
            dma((owned, steps)), dma((owned, steps)),
            dma((owned, 2, steps)), dma((owned, 2, steps)),
            dma((2, n_block, PIECES)), dma((n_block, PIECES)),
            dma((owned, PIECES)), dma((owned, PIECES)),
            dma((2,)), dma((2,)),
            dma((3,)),
        ],
        compiler_params=pltpu.CompilerParams(
            collective_id=0, has_side_effects=True, vmem_limit_bytes=36 * 2**20),
    )(idx, psi_blocks, left_env[:, 0], right_env[:, 0])


def exchanged(psi_blocks, left_env, right_env, right_owner):
    n_block = lax.axis_size("block")
    per_sector = psi_blocks.shape[0]
    capacity = max(2, 2 * per_sector // n_block)
    rows, width = psi_blocks.shape[1], psi_blocks.shape[2]
    here = left_env.shape[0]
    idx = slot_sources(right_owner, per_sector, n_block, capacity)
    dispatch = (
        idx[:, None] == jnp.arange(per_sector, dtype=jnp.int32)[None, :]
    ).astype(jnp.bfloat16)
    blended = jnp.einsum(
        "wik,bkc->wbic", left_env[:, 0],
        lax.all_gather(psi_blocks, "half", axis=1, tiled=True),
        preferred_element_type=jnp.float32,
    ).astype(jnp.bfloat16)
    outgoing = jnp.einsum(
        "sb,wbrc->wsrc", dispatch, blended, preferred_element_type=jnp.float32
    ).astype(jnp.bfloat16)
    outgoing = outgoing.reshape(here, n_block, capacity, rows, width)
    arrived = lax.all_to_all(outgoing, "block", split_axis=1, concat_axis=1, tiled=True)
    arrived = arrived.reshape(here, n_block * capacity, rows, width)
    partial_value = jnp.zeros((n_block * capacity, rows, width), jnp.float32)
    for w in range(here):
        partial_value = partial_value + jnp.einsum(
            "src,cn->srn", arrived[w], right_env[w, 0], preferred_element_type=jnp.float32)
    return lax.psum_scatter(
        partial_value.astype(jnp.bfloat16), "term", scatter_dimension=0, tiled=True)


def solution(mesh):
    in_specs = (
        P(("groups", "block"), "half", None),
        P(("groups", "term"), "block", "half", None),
        P(("groups", "term"), "block", None, None),
        P("groups", None),
    )
    out_specs = P(("groups", "block", "term"), "half", None)
    small = mesh.shape["term"] == 2 and mesh.shape["half"] == 2 and mesh.shape["block"] == 4
    body = owner_computes if small else exchanged
    return jax.shard_map(body, mesh=mesh, in_specs=in_specs, out_specs=out_specs, check_vma=False)
```
